32 devices in a mesh: parts: 2 (over y), slab: 4 (over z), ang: 2 (over x), chan: 2 (over core).
Axes of the slice: x: 2, y: 2, z: 4, core: 2. Of those that a mesh axis runs over, the one named last changes fastest.
Arguments:
- sinogram: bfloat16 [4, 2, 512, 1024], P(('parts', 'chan'), 'ang', 'slab'), parts along dimension 0, may hold values from -6 to 6
- transaxial: bfloat16 [2, 1024, 1024], P('ang', 'slab'), may hold values from -0.1875 to 0.1875
- targets: int32 [2, 64, 1], P('ang'), may hold values from 0 to 3; in each aligned block of 16 rows (0 to 15, 16 to 31, ..., all dimensions but the last counted through in order) at most 8 rows name the same one
- row_shift: float32 [2, 64], P('ang'), may hold values from -2 to 2
- center: float32 [2, 4096], P('ang', 'slab'), may hold values from 0 to 8
- spread: float32 [2, 4096], P('ang', 'slab'), may hold values from 0.5 to 4
- gain: float32 [2, 4096], P('ang', 'slab'), may hold values from 0.1 to 0.4
Outputs:
- volume: float32 [4, 1024, 4096], P(('parts', 'chan'), 'ang', 'slab'), parts along dimension 0
The draws below stay inside these ranges and needn't reach their ends.
There are 2 independent parts, one for each index of `parts`. The reference program is written for one: setup_inputs(seed, part) draws one part's arguments, and reference() takes and returns one part's arrays. A program takes and returns all parts, laid end to end along the dimension named above; an argument that names none is the same for every part. Nothing has to cross between parts.
Inputs may be any that keep to these rules, and one draw needn't show every extreme that they name: `targets`: within one angle, the 16 sub-blocks of one slab device name any one slab at most 8 times, a bound that some block reaches.
All inputs are finite; a program needn't handle non-finite values.
Results may differ from the reference program's by a relative error of at most 0.015.
Values may be sent and summed in bfloat16 or wider, within the bound.
A program may use at most 64 MiB of HBM per device.

```python
import math
import jax
import jax.numpy as jnp
import numpy as np
from jax import lax

U = 1024
X = 1024
SB = 8
CHANNELS = 2
ANGLES = 2
V_ALL = 512
SUBS = 16
CAP = 8
ROWS_DEV = 1024
ROWS = 4096
N_SLAB = 4


def block_levels(rng, shape, shards, smallest, high):
    level = 1.0
    for dim, blocks in shards:
        draws = jax.random.uniform(jax.random.fold_in(jax.random.fold_in(rng, 6), dim), (blocks,), jnp.float32, smallest / len(shards), high / len(shards))
        level = level * jnp.repeat(jnp.exp(draws), shape[dim] // blocks).reshape((-1,) + (1,) * (len(shape) - 1 - dim))
    return level


def routed_block(stream_key, own, number, rows, count, top, most, slope):
    sequence = jax.random.permutation(stream_key, count)
    crowded, usual = portions_of(count, rows * top, most, slope, True), portions_of(count, rows * top, most, slope, False)
    places = jnp.arange(count)

    def named(tallies, rotation):
        used = int((tallies > 0).sum())
        fixed = max(1, used // 4)
        moved = fixed + (places - fixed + rotation * (used - fixed)) % max(1, count - fixed)
        return jnp.zeros((count,), jnp.int32).at[sequence[jnp.where(places < fixed, places, moved)]].set(jnp.asarray(tallies, jnp.int32))

    tallies = jnp.where(number % 4 == 0, named(crowded, number // 4), named(usual, number - number // 4 - 1))
    mixed = jax.random.permutation(jax.random.fold_in(own, 3), count)
    donor, sink = mixed[0:count // 2 * 2:2], mixed[1:count // 2 * 2:2]
    slack = jnp.minimum(tallies[donor] - 1, most - tallies[sink]) // 2
    slack = jnp.where((donor == sequence[0]) | (sink == sequence[0]) | (tallies[sink] == 0), 0, jnp.maximum(slack, 0))
    moved = jax.random.randint(jax.random.fold_in(own, 4), (count // 2,), 0, 1 << 20) % (slack + 1)
    tallies = tallies.at[donor].add(-moved).at[sink].add(moved)
    members = jnp.searchsorted(jnp.cumsum(tallies), jnp.arange(rows * top), side="right").astype(jnp.int32)
    grid = members.reshape(top, rows).T
    grid = grid[jax.random.permutation(jax.random.fold_in(own, 1), rows)]
    rotation = jax.random.randint(jax.random.fold_in(own, 2), (rows, 1), 0, top)
    return jnp.take_along_axis(grid, (jnp.arange(top)[None, :] + rotation) % top, axis=1)


def portions_of(amount, total, reach, lean, full):
    loads = [(1 << 20) // math.isqrt(grade ** lean) + 1 for grade in range(1, amount + 1)]
    largest = reach if full else min(reach, max(-(-total // amount), total * loads[0] // sum(loads)))
    least = 1 if total - largest >= amount - 1 else 0
    holding, spare = [largest] + [least] * (amount - 1), total - largest - least * (amount - 1)
    while spare > 0:
        movable = [i for i in range(1, amount) if holding[i] < largest] or [i for i in range(1, amount) if holding[i] < reach]
        mass, remaining = sum([loads[i] for i in movable]), spare
        for i in movable:
            more = min(reach - holding[i], max(1, remaining * loads[i] // mass), spare)
            holding[i] = holding[i] + more
            spare = spare - more
    return np.array(holding)


def bell_draw(own_key, dims, width, reach, pieces=(), held_as=jnp.bfloat16):
    loudness = block_levels(own_key, dims, pieces, -0.22, 0.18) if pieces else 1.0
    drawn = jax.random.normal(own_key, dims, jnp.float32) * width * loudness
    return jnp.minimum(jnp.maximum(drawn, -reach), reach).astype(held_as)


def setup_inputs(seed: int = 0, part: int = 0) -> dict:
    splits = jax.random.split(jax.random.key(seed), 8)
    part_splits = jax.random.split(jax.random.fold_in(splits[7], part), 8)
    sinogram = bell_draw(part_splits[0], (CHANNELS, ANGLES, V_ALL, U), 1.0, 6.0, ((0, 2), (1, 2), (2, 4)))
    transaxial = bell_draw(splits[1], (ANGLES, X, U), U ** -0.5, 0.1875, ((0, 2), (1, 4)))
    targets_keys = jax.random.split(jax.random.fold_in(splits[2], 1), ANGLES * (N_SLAB * SUBS) // SUBS)
    targets_turns = jax.random.permutation(jax.random.fold_in(splits[2], 3), ANGLES * (N_SLAB * SUBS) // SUBS)
    targets = jax.vmap(lambda own, number: routed_block(jax.random.fold_in(splits[2], 2), own, number, SUBS, N_SLAB, 1, CAP, 2))(targets_keys, targets_turns).reshape((ANGLES, N_SLAB * SUBS, 1))
    row_shift = jnp.clip(jax.random.uniform(splits[3], (ANGLES, N_SLAB * SUBS), jnp.float32, -2.0, 2.0) * block_levels(splits[3], (ANGLES, N_SLAB * SUBS), ((0, 2),), -0.4, 0.0), -2.0, 2.0)
    center = jnp.clip(8.0 * jax.random.uniform(splits[4], (ANGLES, ROWS), jnp.float32) ** block_levels(splits[4], (ANGLES, ROWS), ((0, 2), (1, 4)), -0.2, 0.2), 0.0, 8.0)
    spread = jnp.clip(jnp.exp(math.log(4.0) - 2.0794415 * jax.random.uniform(splits[5], (ANGLES, ROWS), jnp.float32) ** block_levels(splits[5], (ANGLES, ROWS), ((0, 2), (1, 4)), -0.2, 0.2)), 0.5, 4.0)
    gain = jnp.clip(jnp.exp(math.log(0.4) - 1.3862944 * jax.random.uniform(splits[6], (ANGLES, ROWS), jnp.float32) ** block_levels(splits[6], (ANGLES, ROWS), ((0, 2), (1, 4)), -0.2, 0.2)), 0.1, 0.4)
    return {"sinogram": sinogram, "transaxial": transaxial, "targets": targets, "row_shift": row_shift, "center": center, "spread": spread, "gain": gain}


def footprint_tile(local_pos, row_center, row_spread, row_gain):
    offset = (local_pos[None, :] - row_center[:, None]) / row_spread[:, None]
    tile = row_gain[:, None] * lax.rsqrt(row_spread)[:, None] / (1.0 + offset * offset)
    return tile.astype(jnp.bfloat16)

def reference(sinogram, transaxial, targets, row_shift, center, spread, gain):
    volume = jnp.zeros((CHANNELS, X, ROWS), jnp.float32)
    sub_total = N_SLAB * SUBS
    for angle in range(ANGLES):
        table = targets[angle, :, 0].astype(jnp.int32)
        shifts = row_shift[angle]
        centers = center[angle].reshape(N_SLAB, ROWS_DEV)
        spreads = spread[angle].reshape(N_SLAB, ROWS_DEV)
        gains = gain[angle].reshape(N_SLAB, ROWS_DEV)
        angle_rows = sinogram[:, angle]

        def add_sub(accum, index):
            target = table[index]
            start = (index * SB).astype(jnp.int32)
            zero_idx = jnp.zeros((), jnp.int32)
            rows_here = lax.dynamic_slice(angle_rows, (zero_idx, start, zero_idx), (CHANNELS, SB, U))
            local_pos = jnp.arange(SB, dtype=jnp.float32) + 0.5 - shifts[index]
            tile = footprint_tile(local_pos, centers[target], spreads[target], gains[target])
            contrib = jnp.einsum('rv,cvu->cru', tile.astype(jnp.float32), rows_here.astype(jnp.float32))
            current = lax.dynamic_slice(accum, (zero_idx, target, zero_idx, zero_idx), (CHANNELS, 1, ROWS_DEV, U))
            accum = lax.dynamic_update_slice(accum, current + contrib[:, None], (zero_idx, target, zero_idx, zero_idx))
            return (accum, None)
        start_acc = jnp.zeros((CHANNELS, N_SLAB, ROWS_DEV, U), jnp.float32)
        accum, _ = lax.scan(add_sub, start_acc, jnp.arange(sub_total, dtype=jnp.int32))
        axial = accum.astype(jnp.bfloat16).reshape(CHANNELS, ROWS, U)
        for channel in range(CHANNELS):
            part = jnp.dot(transaxial[angle], axial[channel].T, preferred_element_type=jnp.float32).astype(jnp.bfloat16)
            part = lax.optimization_barrier(part)
            volume = volume.at[channel].add(part.astype(jnp.float32))
    return volume
```

```python
import functools

import jax
import jax.numpy as jnp
from jax import lax
from jax.experimental import pallas as pl
from jax.experimental.pallas import tpu as pltpu
from jax.sharding import PartitionSpec as P

MESH = pl.DeviceIdType.MESH
F32 = jnp.float32
BF16 = jnp.bfloat16


def log2(n):
    assert n & (n - 1) == 0
    return n.bit_length() - 1


def iota(shape, dim):
    return lax.broadcasted_iota(jnp.int32, shape, dim)


def keep(mask, value):
    return jnp.where(mask, value, jnp.zeros_like(value))


def kernel(
    nz, na, subs, cap,
    x_ref, w_ref, targets_ref, shift_ref, center_ref, spread_ref, gain_ref,
    g_out, tile_out,
    w_full, send_rows, rows, g_send, g_recv, meta, pos,
    own_sem, row_ss, row_rs, up_ss, down_ss, wz_rs, wy_ss, wy_rs, wc_ss, wc_rs,
    wd_ss, wd_rs, meta_ss, meta_rs, g_ss, g_rs,
):
    p = lax.axis_index("parts")
    z = lax.axis_index("slab")
    a = lax.axis_index("ang")
    c = lax.axis_index("chan")
    v_rows, width = x_ref.shape
    x_block = w_ref.shape[0]
    quarter = x_block // 4
    sub_rows = v_rows // subs
    total = nz * subs
    piece = cap * sub_rows
    slots = nz * piece
    x_part = g_out.shape[0]
    l_sub, l_subs, l_piece = log2(sub_rows), log2(subs), log2(piece)

    barrier = pltpu.get_barrier_semaphore()
    for d in range(1, nz):
        pl.semaphore_signal(
            barrier, inc=1, device_id={"slab": lax.rem(z + d, nz)}, device_id_type=MESH
        )
    for d in range(1, na):
        pl.semaphore_signal(
            barrier, inc=1, device_id={"ang": lax.rem(a + d, na)}, device_id_type=MESH
        )
    pl.semaphore_signal(barrier, inc=1, device_id={"parts": 1 - p}, device_id_type=MESH)
    pl.semaphore_signal(barrier, inc=1, device_id={"chan": 1 - c}, device_id_type=MESH)

    t_col = targets_ref[...].astype(F32)
    eye = iota((total, total), 0) == iota((total, total), 1)
    t_row = jnp.sum(keep(eye, jnp.broadcast_to(t_col, (total, total))), axis=0, keepdims=True)
    meta[a, 0:1, :] = center_ref[...]
    meta[a, 1:2, :] = spread_ref[...]
    meta[a, 2:3, :] = gain_ref[...]
    meta[a, 3:4, 0:total] = t_row
    meta[a, 4:5, 0:total] = shift_ref[...]

    b_of_v = z * subs + (iota((total, v_rows), 1) >> l_sub)
    b_col = iota((total, v_rows), 0)
    t_wide = jnp.broadcast_to(t_col, (total, v_rows))
    t_v = jnp.sum(keep(b_col == b_of_v, t_wide), axis=0, keepdims=True)
    before = (t_wide == t_v) & (b_col >= z * subs) & (b_col < b_of_v)
    rank_v = jnp.sum(before.astype(F32), axis=0, keepdims=True)
    slot = iota((slots, v_rows), 0)
    v_id = iota((slots, v_rows), 1)
    pick = (
        (t_v == (slot >> l_piece).astype(F32))
        & (rank_v == ((slot & (piece - 1)) >> l_sub).astype(F32))
        & ((v_id & (sub_rows - 1)) == (slot & (sub_rows - 1)))
    )
    send_rows[...] = jnp.dot(
        pick.astype(F32).astype(BF16), x_ref[...], preferred_element_type=F32
    ).astype(BF16)

    pl.semaphore_wait(barrier, nz - 1 + na - 1 + 2)

    def weight_slice(s, qp, qc):
        start = pl.multiple_of(s * x_block + (qp * 2 + qc) * quarter, quarter)
        return w_full.at[pl.ds(start, quarter)]

    def weight_copy(s, qp, qc, ss, rs, device, src=None):
        block = weight_slice(s, qp, qc)
        return pltpu.make_async_remote_copy(
            src_ref=block if src is None else src, dst_ref=block,
            send_sem=ss.at[s], recv_sem=rs.at[s], device_id=device, device_id_type=MESH,
        )

    def up(s, src=None):
        return weight_copy(s, p, c, up_ss, wz_rs, {"slab": lax.rem(z + 1, nz)}, src)

    def down(s, src=None):
        return weight_copy(s, p, c, down_ss, wz_rs, {"slab": lax.rem(z + nz - 1, nz)}, src)

    def across(s, qp=p):
        return weight_copy(s, qp, c, wy_ss, wy_rs, {"parts": 1 - p})

    def twin(s, qc=c):
        return weight_copy(s, p, qc, wc_ss, wc_rs, {"chan": 1 - c})

    def twin_far(s, qc=c):
        return weight_copy(s, 1 - p, qc, wd_ss, wd_rs, {"chan": 1 - c})

    own_quarter = w_ref.at[pl.ds(pl.multiple_of((p * 2 + c) * quarter, quarter), quarter)]

    @pl.when(z + 1 < nz)
    def _():
        up(z, own_quarter).start()

    @pl.when(z > 0)
    def _():
        down(z, own_quarter).start()

    def row_copy(src_z, dst_z):
        return pltpu.make_async_remote_copy(
            src_ref=send_rows.at[pl.ds(pl.multiple_of(dst_z * piece, piece), piece)],
            dst_ref=rows.at[pl.ds(pl.multiple_of(src_z * piece, piece), piece)],
            send_sem=row_ss.at[dst_z], recv_sem=row_rs.at[src_z],
            device_id={"slab": dst_z}, device_id_type=MESH,
        )

    for d in range(1, nz):
        row_copy(z, lax.rem(z + d, nz)).start()

    def meta_copy(src_a, dst_a):
        return pltpu.make_async_remote_copy(
            src_ref=meta.at[src_a], dst_ref=meta.at[src_a],
            send_sem=meta_ss.at[dst_a], recv_sem=meta_rs.at[src_a],
            device_id={"ang": dst_a}, device_id_type=MESH,
        )

    for d in range(1, na):
        meta_copy(a, lax.rem(a + d, na)).start()

    own_copy = pltpu.make_async_copy(
        w_ref, w_full.at[pl.ds(pl.multiple_of(z * x_block, x_block), x_block)], own_sem
    )
    own_copy.start()
    mine = pl.ds(pl.multiple_of(z * piece, piece), piece)
    rows[mine, :] = send_rows[mine, :]

    def make_tile(src_a):
        t_r = meta[src_a, 3:4, 0:total]
        s_r = meta[src_a, 4:5, 0:total]
        t_c = jnp.sum(keep(eye, jnp.broadcast_to(t_r, (total, total))), axis=1, keepdims=True)
        b0, b1 = iota((total, total), 0), iota((total, total), 1)
        earlier = (t_c == t_r) & ((b0 >> l_subs) == (b1 >> l_subs)) & (b0 < b1)
        rank = jnp.sum(earlier.astype(F32), axis=0, keepdims=True)
        sl = iota((slots, total), 0)
        b = iota((slots, total), 1)
        match = (
            ((b >> l_subs) == (sl >> l_piece))
            & (t_r == z.astype(F32))
            & (rank == ((sl & (piece - 1)) >> l_sub).astype(F32))
        )
        shift = jnp.sum(keep(match, jnp.broadcast_to(s_r, (slots, total))), axis=1, keepdims=True)
        j = (iota((slots, 1), 0) & (sub_rows - 1)).astype(F32)
        pos[...] = j + 0.5 - shift
        center = meta[src_a, 0:1, :]
        spread = meta[src_a, 1:2, :]
        scale = meta[src_a, 2:3, :] * lax.rsqrt(spread)
        inverse = 1.0 / spread
        step = min(32, slots)

        @pl.loop(0, slots // step)
        def _(i):
            at = pl.multiple_of(i * step, step)
            offset = (pos[pl.ds(at, step), :] - center) * inverse
            tile_out[pl.ds(pl.multiple_of(src_a * slots + at, step), step), :] = (
                scale / (1.0 + offset * offset)
            ).astype(BF16)

    make_tile(a)

    for t in range(1, nz):
        below, above = z - t, z + t

        @pl.when(below >= 0)
        def _():
            up(below).wait_recv()

            @pl.when(z + 1 < nz)
            def _():
                up(below).start()

            across(below).start()
            twin(below).start()

        @pl.when(above < nz)
        def _():
            down(above).wait_recv()

            @pl.when(z > 0)
            def _():
                down(above).start()

            across(above).start()
            twin(above).start()

        for s, there in ((below, below >= 0), (above, above < nz)):
            @pl.when(there)
            def _():
                across(s, 1 - p).wait_recv()
                twin_far(s).start()

    for d in range(1, na):
        src_a = lax.rem(a + d, na)
        meta_copy(src_a, a).wait_recv()
        make_tile(src_a)

    for d in range(1, nz):
        row_copy(lax.rem(z + d, nz), z).wait_recv()
    own_copy.wait()
    for d in range(1, nz):
        s = lax.rem(z + d, nz)
        twin(s, 1 - c).wait_recv()
        twin_far(s, 1 - c).wait_recv()

    def g_copy(src_a, dst_a):
        return pltpu.make_async_remote_copy(
            src_ref=g_send.at[dst_a], dst_ref=g_recv.at[src_a],
            send_sem=g_ss.at[dst_a], recv_sem=g_rs.at[src_a],
            device_id={"ang": dst_a}, device_id_type=MESH,
        )

    x_tile = min(256, x_part)

    def project(dst_a, out):
        @pl.loop(0, x_part // x_tile)
        def _(i):
            at = pl.multiple_of(i * x_tile, x_tile)
            block = w_full[pl.ds(pl.multiple_of(dst_a * x_part + at, x_tile), x_tile), :]
            out[pl.ds(at, x_tile), :] = lax.dot_general(
                block, rows[...], (((1,), (1,)), ((), ())), preferred_element_type=F32
            ).astype(BF16)

    for d in range(1, na):
        dst_a = lax.rem(a + d, na)
        project(dst_a, g_send.at[dst_a])
        g_copy(a, dst_a).start()
    project(a, g_recv.at[a])

    for d in range(1, na):
        g_copy(lax.rem(a + d, na), a).wait_recv()
    for k in range(na):
        g_out[:, k * slots:(k + 1) * slots] = g_recv[k]

    for d in range(1, nz):
        row_copy(z, lax.rem(z + d, nz)).wait_send()
    for d in range(1, na):
        meta_copy(a, lax.rem(a + d, na)).wait_send()
        g_copy(a, lax.rem(a + d, na)).wait_send()
    for s in range(nz):
        @pl.when((s <= z) & (z + 1 < nz))
        def _():
            up(s).wait_send()

        @pl.when((s >= z) & (z > 0))
        def _():
            down(s).wait_send()

        @pl.when(s != z)
        def _():
            across(s).wait_send()
            twin(s).wait_send()
            twin_far(s).wait_send()


def shards(sinogram, transaxial, targets, row_shift, center, spread, gain):
    nz = lax.axis_size("slab")
    na = lax.axis_size("ang")
    detector = sinogram[0, 0]
    weights = transaxial[0]
    v_rows, width = detector.shape
    total = targets.shape[1]
    subs = total // nz
    sub_rows = v_rows // subs
    cap = max(2, 2 * subs // nz)
    piece = cap * sub_rows
    slots = nz * piece
    x_all = weights.shape[0] * nz
    x_part = x_all // na
    r_rows = center.shape[1]
    vmem = pl.BlockSpec(memory_space=pltpu.VMEM)
    dma = pltpu.SemaphoreType.DMA
    projected, tile = pl.pallas_call(
        functools.partial(kernel, nz, na, subs, cap),
        out_shape=(
            jax.ShapeDtypeStruct((x_part, na * slots), BF16),
            jax.ShapeDtypeStruct((na * slots, r_rows), BF16),
        ),
        in_specs=[vmem, pl.BlockSpec(memory_space=pl.ANY)] + [vmem] * 5,
        out_specs=(vmem, vmem),
        scratch_shapes=[
            pltpu.VMEM((x_all, width), BF16),
            pltpu.VMEM((slots, width), BF16),
            pltpu.VMEM((slots, width), BF16),
            pltpu.VMEM((na, x_part, slots), BF16),
            pltpu.VMEM((na, x_part, slots), BF16),
            pltpu.VMEM((na, 8, r_rows), F32),
            pltpu.VMEM((slots, 1), F32),
            dma(()),
        ] + [dma((nz,))] * 11 + [dma((na,))] * 4,
        compiler_params=pltpu.CompilerParams(
            collective_id=0, has_side_effects=True, vmem_limit_bytes=32 * 1024 * 1024
        ),
    )(detector, weights, targets[0], row_shift, center, spread, gain)
    volume = jnp.dot(projected, tile, preferred_element_type=F32)
    return volume[None]


def solution(mesh):
    assert mesh.shape["parts"] == 2 and mesh.shape["chan"] == 2
    in_specs = (
        P(("parts", "chan"), "ang", "slab", None),
        P("ang", "slab", None),
        P("ang", None, None),
        P("ang", None),
        P("ang", "slab"),
        P("ang", "slab"),
        P("ang", "slab"),
    )
    out_specs = P(("parts", "chan"), "ang", "slab")
    return jax.shard_map(shards, mesh=mesh, in_specs=in_specs, out_specs=out_specs, check_vma=False)
```

```python
import functools

import jax
import jax.numpy as jnp
from jax import lax
from jax.experimental import pallas as pl
from jax.experimental.pallas import tpu as pltpu
from jax.sharding import PartitionSpec as P

MESH = pl.DeviceIdType.MESH
F32 = jnp.float32
BF16 = jnp.bfloat16


def log2(n):
    assert n & (n - 1) == 0
    return n.bit_length() - 1


def iota(shape, dim):
    return lax.broadcasted_iota(jnp.int32, shape, dim)


def keep(mask, value):
    return jnp.where(mask, value, jnp.zeros_like(value))


def kernel(
    nz, na, subs, cap,
    x_hbm, w_ref, targets_hbm, shift_hbm, center_hbm, spread_hbm, gain_hbm,
    g_out, tile_out,
    x_ref, targets_ref, shift_ref, center_ref, spread_ref, gain_ref,
    w_full, send_rows, rows, w_proj, g_recv, meta, pos,
    in_sem, own_sem, row_ss, row_rs, up_ss, down_ss, wz_rs, wy_ss, wy_rs, wc_ss, wc_rs,
    wd_ss, wd_rs, meta_ss, meta_rs, g_ss, g_rs,
):
    p = lax.axis_index("parts")
    z = lax.axis_index("slab")
    a = lax.axis_index("ang")
    c = lax.axis_index("chan")
    inputs = [
        pltpu.make_async_copy(src, dst, in_sem.at[i])
        for i, (src, dst) in enumerate((
            (targets_hbm, targets_ref), (shift_hbm, shift_ref), (center_hbm, center_ref),
            (spread_hbm, spread_ref), (gain_hbm, gain_ref), (x_hbm, x_ref),
        ))
    ]
    for copy in inputs:
        copy.start()
    v_rows, width = x_ref.shape
    x_block = w_ref.shape[0]
    quarter = x_block // 4
    sub_rows = v_rows // subs
    total = nz * subs
    piece = cap * sub_rows
    slots = nz * piece
    x_part = g_out.shape[0]
    l_sub, l_subs, l_piece = log2(sub_rows), log2(subs), log2(piece)

    barrier = pltpu.get_barrier_semaphore()
    for d in range(1, nz):
        pl.semaphore_signal(
            barrier, inc=1, device_id={"slab": lax.rem(z + d, nz)}, device_id_type=MESH
        )
    for d in range(1, na):
        pl.semaphore_signal(
            barrier, inc=1, device_id={"ang": lax.rem(a + d, na)}, device_id_type=MESH
        )
    pl.semaphore_signal(barrier, inc=1, device_id={"parts": 1 - p}, device_id_type=MESH)
    pl.semaphore_signal(barrier, inc=1, device_id={"chan": 1 - c}, device_id_type=MESH)

    pl.semaphore_wait(barrier, nz - 1 + na - 1 + 2)

    def weight_slice(s, qp, qc):
        start = pl.multiple_of(s * x_block + (qp * 2 + qc) * quarter, quarter)
        return w_full.at[pl.ds(start, quarter)]

    def weight_copy(s, qp, qc, ss, rs, device, src=None):
        block = weight_slice(s, qp, qc)
        return pltpu.make_async_remote_copy(
            src_ref=block if src is None else src, dst_ref=block,
            send_sem=ss.at[s], recv_sem=rs.at[s], device_id=device, device_id_type=MESH,
        )

    def up(s, src=None):
        return weight_copy(s, p, c, up_ss, wz_rs, {"slab": lax.rem(z + 1, nz)}, src)

    def down(s, src=None):
        return weight_copy(s, p, c, down_ss, wz_rs, {"slab": lax.rem(z + nz - 1, nz)}, src)

    def across(s, qp=p):
        return weight_copy(s, qp, c, wy_ss, wy_rs, {"parts": 1 - p})

    def twin(s, qc=c):
        return weight_copy(s, p, qc, wc_ss, wc_rs, {"chan": 1 - c})

    def twin_far(s, qc=c):
        return weight_copy(s, 1 - p, qc, wd_ss, wd_rs, {"chan": 1 - c})

    own_quarter = w_ref.at[pl.ds(pl.multiple_of((p * 2 + c) * quarter, quarter), quarter)]

    @pl.when(z + 1 < nz)
    def _():
        up(z, own_quarter).start()

    @pl.when(z > 0)
    def _():
        down(z, own_quarter).start()

    own_copy = pltpu.make_async_copy(
        w_ref, w_full.at[pl.ds(pl.multiple_of(z * x_block, x_block), x_block)], own_sem
    )
    own_copy.start()

    for copy in inputs[:-1]:
        copy.wait()
    t_row = targets_ref[...].astype(F32)
    eye = iota((total, total), 0) == iota((total, total), 1)
    t_col = jnp.sum(keep(eye, jnp.broadcast_to(t_row, (total, total))), axis=1, keepdims=True)
    meta[a, 0:1, :] = center_ref[...]
    meta[a, 1:2, :] = spread_ref[...]
    meta[a, 2:3, :] = gain_ref[...]
    meta[a, 3:4, 0:total] = t_row
    meta[a, 4:5, 0:total] = shift_ref[...]

    b_of_v = z * subs + (iota((total, v_rows), 1) >> l_sub)
    b_col = iota((total, v_rows), 0)
    t_wide = jnp.broadcast_to(t_col, (total, v_rows))
    t_v = jnp.sum(keep(b_col == b_of_v, t_wide), axis=0, keepdims=True)
    before = (t_wide == t_v) & (b_col >= z * subs) & (b_col < b_of_v)
    rank_v = jnp.sum(before.astype(F32), axis=0, keepdims=True)
    slot = iota((slots, v_rows), 0)
    v_id = iota((slots, v_rows), 1)
    pick = (
        (t_v == (slot >> l_piece).astype(F32))
        & (rank_v == ((slot & (piece - 1)) >> l_sub).astype(F32))
        & ((v_id & (sub_rows - 1)) == (slot & (sub_rows - 1)))
    )
    inputs[-1].wait()
    send_rows[...] = jnp.dot(
        pick.astype(F32).astype(BF16), x_ref[...], preferred_element_type=F32
    ).astype(BF16)

    def make_tile(src_a):
        t_r = meta[src_a, 3:4, 0:total]
        s_r = meta[src_a, 4:5, 0:total]
        t_c = jnp.sum(keep(eye, jnp.broadcast_to(t_r, (total, total))), axis=1, keepdims=True)
        b0, b1 = iota((total, total), 0), iota((total, total), 1)
        earlier = (t_c == t_r) & ((b0 >> l_subs) == (b1 >> l_subs)) & (b0 < b1)
        rank = jnp.sum(earlier.astype(F32), axis=0, keepdims=True)
        sl = iota((slots, total), 0)
        b = iota((slots, total), 1)
        match = (
            ((b >> l_subs) == (sl >> l_piece))
            & (t_r == z.astype(F32))
            & (rank == ((sl & (piece - 1)) >> l_sub).astype(F32))
        )
        shift = jnp.sum(keep(match, jnp.broadcast_to(s_r, (slots, total))), axis=1, keepdims=True)
        j = (iota((slots, 1), 0) & (sub_rows - 1)).astype(F32)
        pos[...] = j + 0.5 - shift
        center = meta[src_a, 0:1, :]
        spread = meta[src_a, 1:2, :]
        scale = meta[src_a, 2:3, :] * lax.rsqrt(spread)
        inverse = 1.0 / spread
        step = min(32, slots)

        @pl.loop(0, slots // step)
        def _(i):
            at = pl.multiple_of(i * step, step)
            offset = (pos[pl.ds(at, step), :] - center) * inverse
            tile_out[pl.ds(pl.multiple_of(src_a * slots + at, step), step), :] = (
                scale / (1.0 + offset * offset)
            ).astype(BF16)

    def row_copy(src_z, dst_z):
        return pltpu.make_async_remote_copy(
            src_ref=send_rows.at[pl.ds(pl.multiple_of(dst_z * piece, piece), piece)],
            dst_ref=rows.at[pl.ds(pl.multiple_of(src_z * piece, piece), piece)],
            send_sem=row_ss.at[dst_z], recv_sem=row_rs.at[src_z],
            device_id={"slab": dst_z}, device_id_type=MESH,
        )

    row_copy(z, lax.rem(z + nz // 2, nz)).start()

    def meta_copy(src_a, dst_a):
        return pltpu.make_async_remote_copy(
            src_ref=meta.at[src_a], dst_ref=meta.at[src_a],
            send_sem=meta_ss.at[dst_a], recv_sem=meta_rs.at[src_a],
            device_id={"ang": dst_a}, device_id_type=MESH,
        )

    for d in range(1, na):
        meta_copy(a, lax.rem(a + d, na)).start()

    mine = pl.ds(pl.multiple_of(z * piece, piece), piece)
    rows[mine, :] = send_rows[mine, :]

    make_tile(a)
    for d in range(1, na):
        src_a = lax.rem(a + d, na)
        meta_copy(src_a, a).wait_recv()
        make_tile(src_a)


    parts_of = nz // na

    def g_copy(s, src_a, dst_a):
        at = pl.multiple_of(lax.rem(s, parts_of) * x_block, x_block)
        return pltpu.make_async_remote_copy(
            src_ref=w_proj.at[pl.ds(pl.multiple_of(s * x_block, x_block), x_block)],
            dst_ref=g_recv.at[src_a, pl.ds(at, x_block)],
            send_sem=g_ss.at[s], recv_sem=g_rs.at[src_a * parts_of + lax.rem(s, parts_of)],
            device_id={"ang": dst_a}, device_id_type=MESH,
        )

    def project(s):
        at = pl.ds(pl.multiple_of(s * x_block, x_block), x_block)
        block = lax.dot_general(
            w_full[at, :], rows[...], (((1,), (1,)), ((), ())), preferred_element_type=F32
        ).astype(BF16)
        dst_a = s // parts_of

        @pl.when(dst_a != a)
        def _():
            w_proj[at, :] = block
            g_copy(s, a, dst_a).start()

        @pl.when(dst_a == a)
        def _():
            g_recv[
                a, pl.ds(pl.multiple_of(lax.rem(s, parts_of) * x_block, x_block), x_block), :
            ] = block

    pace = [d for d in range(1, nz) if d != nz // 2]
    for t in range(1, nz + 2):
        if t < nz:
            below, above = z - t, z + t

            @pl.when(below >= 0)
            def _():
                up(below).wait_recv()

                @pl.when(z + 1 < nz)
                def _():
                    up(below).start()

                across(below).start()
                twin(below).start()

            @pl.when(above < nz)
            def _():
                down(above).wait_recv()

                @pl.when(z > 0)
                def _():
                    down(above).start()

                across(above).start()
                twin(above).start()

            if t == 1:
                for d in pace:
                    row_copy(z, lax.rem(z + d, nz)).start()
        if 1 < t <= nz:
            for s in (z - t + 1, z + t - 1):
                @pl.when((s >= 0) & (s < nz))
                def _():
                    across(s, 1 - p).wait_recv()
                    twin_far(s).start()
        if t == 2:
            for d in range(1, nz):
                row_copy(lax.rem(z + d, nz), z).wait_recv()
            own_copy.wait()
            project(z)
        if t > 2:
            for s in (z - t + 2, z + t - 2):
                @pl.when((s >= 0) & (s < nz))
                def _():
                    twin(s, 1 - c).wait_recv()
                    twin_far(s, 1 - c).wait_recv()
                    project(s)

    for d in range(1, na):
        src_a = lax.rem(a + d, na)
        for k in range(parts_of):
            g_copy(a * parts_of + k, src_a, a).wait_recv()
    for k in range(na):
        g_out[:, k * slots:(k + 1) * slots] = g_recv[k]

    for d in range(1, nz):
        row_copy(z, lax.rem(z + d, nz)).wait_send()
    for d in range(1, na):
        meta_copy(a, lax.rem(a + d, na)).wait_send()
    for s in range(nz):
        @pl.when(s // parts_of != a)
        def _():
            g_copy(s, a, s // parts_of).wait_send()

        @pl.when((s <= z) & (z + 1 < nz))
        def _():
            up(s).wait_send()

        @pl.when((s >= z) & (z > 0))
        def _():
            down(s).wait_send()

        @pl.when(s != z)
        def _():
            across(s).wait_send()
            twin(s).wait_send()
            twin_far(s).wait_send()


def shards(sinogram, transaxial, targets, row_shift, center, spread, gain):
    nz = lax.axis_size("slab")
    na = lax.axis_size("ang")
    detector = sinogram[0, 0]
    weights = transaxial[0]
    v_rows, width = detector.shape
    total = targets.shape[1]
    subs = total // nz
    sub_rows = v_rows // subs
    cap = max(2, 2 * subs // nz)
    piece = cap * sub_rows
    slots = nz * piece
    x_all = weights.shape[0] * nz
    x_part = x_all // na
    r_rows = center.shape[1]
    vmem = pl.BlockSpec(memory_space=pltpu.VMEM)
    dma = pltpu.SemaphoreType.DMA
    projected, tile = pl.pallas_call(
        functools.partial(kernel, nz, na, subs, cap),
        out_shape=(
            jax.ShapeDtypeStruct((x_part, na * slots), BF16),
            jax.ShapeDtypeStruct((na * slots, r_rows), BF16),
        ),
        in_specs=[pl.BlockSpec(memory_space=pl.ANY)] * 7,
        out_specs=(vmem, vmem),
        scratch_shapes=[
            pltpu.VMEM((v_rows, width), BF16),
            pltpu.VMEM((1, total), jnp.int32),
            pltpu.VMEM((1, total), F32),
            pltpu.VMEM((1, r_rows), F32),
            pltpu.VMEM((1, r_rows), F32),
            pltpu.VMEM((1, r_rows), F32),
            pltpu.VMEM((x_all, width), BF16),
            pltpu.VMEM((slots, width), BF16),
            pltpu.VMEM((slots, width), BF16),
            pltpu.VMEM((x_all, slots), BF16),
            pltpu.VMEM((na, x_part, slots), BF16),
            pltpu.VMEM((na, 8, r_rows), F32),
            pltpu.VMEM((slots, 1), F32),
            dma((6,)),
            dma(()),
        ] + [dma((nz,))] * 11 + [dma((na,))] * 2 + [dma((nz,))] * 2,
        compiler_params=pltpu.CompilerParams(
            collective_id=0, has_side_effects=True, vmem_limit_bytes=60 * 1024 * 1024
        ),
    )(detector, weights, targets[..., 0], row_shift, center, spread, gain)
    volume = jnp.dot(projected, tile, preferred_element_type=F32)
    return volume[None]


def solution(mesh):
    assert mesh.shape["parts"] == 2 and mesh.shape["chan"] == 2
    in_specs = (
        P(("parts", "chan"), "ang", "slab", None),
        P("ang", "slab", None),
        P("ang", None, None),
        P("ang", None),
        P("ang", "slab"),
        P("ang", "slab"),
        P("ang", "slab"),
    )
    out_specs = P(("parts", "chan"), "ang", "slab")
    return jax.shard_map(shards, mesh=mesh, in_specs=in_specs, out_specs=out_specs, check_vma=False)
```

```python
import functools

import jax
import jax.numpy as jnp
from jax import lax
from jax.experimental import pallas as pl
from jax.experimental.pallas import tpu as pltpu
from jax.sharding import PartitionSpec as P

MESH = pl.DeviceIdType.MESH
F32 = jnp.float32
BF16 = jnp.bfloat16


def log2(n):
    assert n & (n - 1) == 0
    return n.bit_length() - 1


def iota(shape, dim):
    return lax.broadcasted_iota(jnp.int32, shape, dim)


def keep(mask, value):
    return jnp.where(mask, value, jnp.zeros_like(value))


def kernel(
    nz, na, subs, cap, halves,
    x_hbm, w_ref, targets_hbm, shift_hbm, center_hbm, spread_hbm, gain_hbm,
    g_out, tile_out,
    x_ref, targets_ref, shift_ref, center_ref, spread_ref, gain_ref,
    w_full, send_rows, rows, w_proj, g_recv, meta, pos,
    in_sem, own_sem, row_ss, row_rs, up_ss, down_ss, wz_rs, wy_ss, wy_rs, wc_ss, wc_rs,
    wd_ss, wd_rs, meta_ss, meta_rs, g_ss, g_rs,
):
    p = lax.axis_index("parts")
    z = lax.axis_index("slab")
    a = lax.axis_index("ang")
    c = lax.axis_index("chan")
    inputs = [
        pltpu.make_async_copy(src, dst, in_sem.at[i])
        for i, (src, dst) in enumerate((
            (targets_hbm, targets_ref), (shift_hbm, shift_ref), (center_hbm, center_ref),
            (spread_hbm, spread_ref), (gain_hbm, gain_ref), (x_hbm, x_ref),
        ))
    ]
    for copy in inputs:
        copy.start()
    v_rows, width = x_ref.shape
    x_block = w_ref.shape[0]
    x_half = x_block // halves
    grain = x_half // 4
    sub_rows = v_rows // subs
    total = nz * subs
    piece = cap * sub_rows
    slots = nz * piece
    x_part = g_out.shape[0]
    l_sub, l_subs, l_piece = log2(sub_rows), log2(subs), log2(piece)

    barrier = pltpu.get_barrier_semaphore()
    for d in range(1, nz):
        pl.semaphore_signal(
            barrier, inc=1, device_id={"slab": lax.rem(z + d, nz)}, device_id_type=MESH
        )
    for d in range(1, na):
        pl.semaphore_signal(
            barrier, inc=1, device_id={"ang": lax.rem(a + d, na)}, device_id_type=MESH
        )
    pl.semaphore_signal(barrier, inc=1, device_id={"parts": 1 - p}, device_id_type=MESH)
    pl.semaphore_signal(barrier, inc=1, device_id={"chan": 1 - c}, device_id_type=MESH)

    pl.semaphore_wait(barrier, nz - 1 + na - 1 + 2)

    def weight_copy(s, h, qp, qc, ss, rs, device, src=None):
        start = s * x_block + h * x_half + (qp * 2 + qc) * grain
        block = w_full.at[pl.ds(pl.multiple_of(start, grain), grain)]
        return pltpu.make_async_remote_copy(
            src_ref=block if src is None else src, dst_ref=block,
            send_sem=ss.at[s * halves + h], recv_sem=rs.at[s * halves + h],
            device_id=device, device_id_type=MESH,
        )

    def up(s, h, src=None):
        return weight_copy(s, h, p, c, up_ss, wz_rs, {"slab": lax.rem(z + 1, nz)}, src)

    def down(s, h, src=None):
        return weight_copy(s, h, p, c, down_ss, wz_rs, {"slab": lax.rem(z + nz - 1, nz)}, src)

    def across(s, h, qp=p):
        return weight_copy(s, h, qp, c, wy_ss, wy_rs, {"parts": 1 - p})

    def twin(s, h, qc=c):
        return weight_copy(s, h, p, qc, wc_ss, wc_rs, {"chan": 1 - c})

    def twin_far(s, h, qc=c):
        return weight_copy(s, h, 1 - p, qc, wd_ss, wd_rs, {"chan": 1 - c})

    for h in range(halves):
        start = h * x_half + (p * 2 + c) * grain
        own = w_ref.at[pl.ds(pl.multiple_of(start, grain), grain)]

        @pl.when(z + 1 < nz)
        def _():
            up(z, h, own).start()

        @pl.when(z > 0)
        def _():
            down(z, h, own).start()

    own_copy = pltpu.make_async_copy(
        w_ref, w_full.at[pl.ds(pl.multiple_of(z * x_block, x_block), x_block)], own_sem
    )
    own_copy.start()

    for copy in inputs[:-1]:
        copy.wait()
    t_row = targets_ref[...].astype(F32)
    eye = iota((total, total), 0) == iota((total, total), 1)
    t_col = jnp.sum(keep(eye, jnp.broadcast_to(t_row, (total, total))), axis=1, keepdims=True)
    meta[a, 0:1, :] = center_ref[...]
    meta[a, 1:2, :] = spread_ref[...]
    meta[a, 2:3, :] = gain_ref[...]
    meta[a, 3:4, 0:total] = t_row
    meta[a, 4:5, 0:total] = shift_ref[...]

    b_of_v = z * subs + (iota((total, v_rows), 1) >> l_sub)
    b_col = iota((total, v_rows), 0)
    t_wide = jnp.broadcast_to(t_col, (total, v_rows))
    t_v = jnp.sum(keep(b_col == b_of_v, t_wide), axis=0, keepdims=True)
    before = (t_wide == t_v) & (b_col >= z * subs) & (b_col < b_of_v)
    rank_v = jnp.sum(before.astype(F32), axis=0, keepdims=True)
    slot = iota((slots, v_rows), 0)
    v_id = iota((slots, v_rows), 1)
    pick = (
        (t_v == (slot >> l_piece).astype(F32))
        & (rank_v == ((slot & (piece - 1)) >> l_sub).astype(F32))
        & ((v_id & (sub_rows - 1)) == (slot & (sub_rows - 1)))
    )
    inputs[-1].wait()
    send_rows[...] = jnp.dot(
        pick.astype(F32).astype(BF16), x_ref[...], preferred_element_type=F32
    ).astype(BF16)

    def make_tile(src_a):
        t_r = meta[src_a, 3:4, 0:total]
        s_r = meta[src_a, 4:5, 0:total]
        t_c = jnp.sum(keep(eye, jnp.broadcast_to(t_r, (total, total))), axis=1, keepdims=True)
        b0, b1 = iota((total, total), 0), iota((total, total), 1)
        earlier = (t_c == t_r) & ((b0 >> l_subs) == (b1 >> l_subs)) & (b0 < b1)
        rank = jnp.sum(earlier.astype(F32), axis=0, keepdims=True)
        sl = iota((slots, total), 0)
        b = iota((slots, total), 1)
        match = (
            ((b >> l_subs) == (sl >> l_piece))
            & (t_r == z.astype(F32))
            & (rank == ((sl & (piece - 1)) >> l_sub).astype(F32))
        )
        shift = jnp.sum(keep(match, jnp.broadcast_to(s_r, (slots, total))), axis=1, keepdims=True)
        j = (iota((slots, 1), 0) & (sub_rows - 1)).astype(F32)
        pos[...] = j + 0.5 - shift
        center = meta[src_a, 0:1, :]
        spread = meta[src_a, 1:2, :]
        scale = meta[src_a, 2:3, :] * lax.rsqrt(spread)
        inverse = 1.0 / spread
        step = min(32, slots)

        @pl.loop(0, slots // step)
        def _(i):
            at = pl.multiple_of(i * step, step)
            offset = (pos[pl.ds(at, step), :] - center) * inverse
            tile_out[pl.ds(pl.multiple_of(src_a * slots + at, step), step), :] = (
                scale / (1.0 + offset * offset)
            ).astype(BF16)

    def row_copy(src_z, dst_z):
        return pltpu.make_async_remote_copy(
            src_ref=send_rows.at[pl.ds(pl.multiple_of(dst_z * piece, piece), piece)],
            dst_ref=rows.at[pl.ds(pl.multiple_of(src_z * piece, piece), piece)],
            send_sem=row_ss.at[dst_z], recv_sem=row_rs.at[src_z],
            device_id={"slab": dst_z}, device_id_type=MESH,
        )

    row_copy(z, lax.rem(z + nz // 2, nz)).start()

    def meta_copy(src_a, dst_a):
        return pltpu.make_async_remote_copy(
            src_ref=meta.at[src_a], dst_ref=meta.at[src_a],
            send_sem=meta_ss.at[dst_a], recv_sem=meta_rs.at[src_a],
            device_id={"ang": dst_a}, device_id_type=MESH,
        )

    for d in range(1, na):
        meta_copy(a, lax.rem(a + d, na)).start()

    mine = pl.ds(pl.multiple_of(z * piece, piece), piece)
    rows[mine, :] = send_rows[mine, :]

    make_tile(a)
    for d in range(1, na):
        src_a = lax.rem(a + d, na)
        meta_copy(src_a, a).wait_recv()
        make_tile(src_a)


    parts_of = nz // na

    def g_copy(s, h, src_a, dst_a):
        near = lax.rem(s, parts_of)
        at = pl.multiple_of(near * x_block + h * x_half, x_half)
        return pltpu.make_async_remote_copy(
            src_ref=w_proj.at[pl.ds(pl.multiple_of(s * x_block + h * x_half, x_half), x_half)],
            dst_ref=g_recv.at[src_a, pl.ds(at, x_half)],
            send_sem=g_ss.at[s * halves + h],
            recv_sem=g_rs.at[(src_a * parts_of + near) * halves + h],
            device_id={"ang": dst_a}, device_id_type=MESH,
        )

    def project(s, h):
        at = pl.ds(pl.multiple_of(s * x_block + h * x_half, x_half), x_half)
        block = lax.dot_general(
            w_full[at, :], rows[...], (((1,), (1,)), ((), ())), preferred_element_type=F32
        ).astype(BF16)
        dst_a = s // parts_of

        @pl.when(dst_a != a)
        def _():
            w_proj[at, :] = block
            g_copy(s, h, a, dst_a).start()

        @pl.when(dst_a == a)
        def _():
            here = lax.rem(s, parts_of) * x_block + h * x_half
            g_recv[a, pl.ds(pl.multiple_of(here, x_half), x_half), :] = block

    pace = [d for d in range(nz - 1, 0, -1) if d != nz // 2]
    def pass_on(t, h):
        below, above = z - t, z + t

        @pl.when(below >= 0)
        def _():
            up(below, h).wait_recv()

            @pl.when(z + 1 < nz)
            def _():
                up(below, h).start()

            across(below, h).start()
            twin(below, h).start()

        @pl.when(above < nz)
        def _():
            down(above, h).wait_recv()

            @pl.when(z > 0)
            def _():
                down(above, h).start()

            across(above, h).start()
            twin(above, h).start()

    def pass_to_twin(t, h):
        for s in (z - t, z + t):
            @pl.when((s >= 0) & (s < nz))
            def _():
                across(s, h, 1 - p).wait_recv()
                twin_far(s, h).start()

    def finish(t, h):
        for s in (z - t, z + t):
            @pl.when((s >= 0) & (s < nz))
            def _():
                twin(s, h, 1 - c).wait_recv()
                twin_far(s, h, 1 - c).wait_recv()
                project(s, h)

    steps = [(t, h) for t in range(1, nz) for h in range(halves)]
    ready = 2 * halves - 1
    done = 0
    for i, step in enumerate(steps):
        pass_on(*step)
        if i == halves - 1:
            for d in pace:
                row_copy(z, lax.rem(z + d, nz)).start()
        if i:
            pass_to_twin(*steps[i - 1])
        if i == ready:
            for d in range(1, nz):
                row_copy(lax.rem(z + d, nz), z).wait_recv()
            own_copy.wait()
            for h in range(halves):
                project(z, h)
        if i >= ready:
            while done < i - 1:
                finish(*steps[done])
                done += 1
    pass_to_twin(*steps[-1])
    for step in steps[done:]:
        finish(*step)

    for d in range(1, na):
        src_a = lax.rem(a + d, na)
        for k in range(parts_of):
            for h in range(halves):
                g_copy(a * parts_of + k, h, src_a, a).wait_recv()
    for k in range(na):
        g_out[:, k * slots:(k + 1) * slots] = g_recv[k]

    for d in range(1, nz):
        row_copy(z, lax.rem(z + d, nz)).wait_send()
    for d in range(1, na):
        meta_copy(a, lax.rem(a + d, na)).wait_send()
    for s in range(nz):
        @pl.when(s // parts_of != a)
        def _():
            for h in range(halves):
                g_copy(s, h, a, s // parts_of).wait_send()

        for h in range(halves):
            @pl.when((s <= z) & (z + 1 < nz))
            def _():
                up(s, h).wait_send()

            @pl.when((s >= z) & (z > 0))
            def _():
                down(s, h).wait_send()

            @pl.when(s != z)
            def _():
                across(s, h).wait_send()
                twin(s, h).wait_send()
                twin_far(s, h).wait_send()


def shards(sinogram, transaxial, targets, row_shift, center, spread, gain):
    nz = lax.axis_size("slab")
    na = lax.axis_size("ang")
    detector = sinogram[0, 0]
    weights = transaxial[0]
    v_rows, width = detector.shape
    total = targets.shape[1]
    subs = total // nz
    sub_rows = v_rows // subs
    cap = max(2, 2 * subs // nz)
    piece = cap * sub_rows
    slots = nz * piece
    x_all = weights.shape[0] * nz
    x_part = x_all // na
    r_rows = center.shape[1]
    halves = max(1, min(2, weights.shape[0] // 4 // 16))
    vmem = pl.BlockSpec(memory_space=pltpu.VMEM)
    dma = pltpu.SemaphoreType.DMA
    projected, tile = pl.pallas_call(
        functools.partial(kernel, nz, na, subs, cap, halves),
        out_shape=(
            jax.ShapeDtypeStruct((x_part, na * slots), BF16),
            jax.ShapeDtypeStruct((na * slots, r_rows), BF16),
        ),
        in_specs=[pl.BlockSpec(memory_space=pl.ANY)] * 7,
        out_specs=(vmem, vmem),
        scratch_shapes=[
            pltpu.VMEM((v_rows, width), BF16),
            pltpu.VMEM((1, total), jnp.int32),
            pltpu.VMEM((1, total), F32),
            pltpu.VMEM((1, r_rows), F32),
            pltpu.VMEM((1, r_rows), F32),
            pltpu.VMEM((1, r_rows), F32),
            pltpu.VMEM((x_all, width), BF16),
            pltpu.VMEM((slots, width), BF16),
            pltpu.VMEM((slots, width), BF16),
            pltpu.VMEM((x_all, slots), BF16),
            pltpu.VMEM((na, x_part, slots), BF16),
            pltpu.VMEM((na, 8, r_rows), F32),
            pltpu.VMEM((slots, 1), F32),
            dma((6,)),
            dma(()),
        ] + [dma((nz,))] * 2 + [dma((nz * halves,))] * 9 + [dma((na,))] * 2 + [dma((nz * halves,))] * 2,
        compiler_params=pltpu.CompilerParams(
            collective_id=0, has_side_effects=True, vmem_limit_bytes=60 * 1024 * 1024
        ),
    )(detector, weights, targets[..., 0], row_shift, center, spread, gain)
    volume = jnp.dot(projected, tile, preferred_element_type=F32)
    return volume[None]


def solution(mesh):
    assert mesh.shape["parts"] == 2 and mesh.shape["chan"] == 2
    in_specs = (
        P(("parts", "chan"), "ang", "slab", None),
        P("ang", "slab", None),
        P("ang", None, None),
        P("ang", None),
        P("ang", "slab"),
        P("ang", "slab"),
        P("ang", "slab"),
    )
    out_specs = P(("parts", "chan"), "ang", "slab")
    return jax.shard_map(shards, mesh=mesh, in_specs=in_specs, out_specs=out_specs, check_vma=False)
```

```python
import functools

import jax
import jax.numpy as jnp
from jax import lax
from jax.experimental import pallas as pl
from jax.experimental.pallas import tpu as pltpu
from jax.sharding import PartitionSpec as P

MESH = pl.DeviceIdType.MESH
F32 = jnp.float32
BF16 = jnp.bfloat16


def log2(n):
    assert n & (n - 1) == 0
    return n.bit_length() - 1


def iota(shape, dim):
    return lax.broadcasted_iota(jnp.int32, shape, dim)


def keep(mask, value):
    return jnp.where(mask, value, jnp.zeros_like(value))


def kernel(
    nz, na, subs, cap, halves,
    x_hbm, w_ref, targets_hbm, shift_hbm, center_hbm, spread_hbm, gain_hbm,
    g_out, tile_out,
    x_ref, targets_ref, shift_ref, center_ref, spread_ref, gain_ref,
    w_full, send_rows, rows, w_proj, g_recv, meta, pos,
    in_sem, own_sem, row_ss, row_rs, up_ss, down_ss, wz_rs, wy_ss, wy_rs, wc_ss, wc_rs,
    wd_ss, wd_rs, meta_ss, meta_rs, g_ss, g_rs,
):
    p = lax.axis_index("parts")
    z = lax.axis_index("slab")
    a = lax.axis_index("ang")
    c = lax.axis_index("chan")
    inputs = [
        pltpu.make_async_copy(src, dst, in_sem.at[i])
        for i, (src, dst) in enumerate((
            (targets_hbm, targets_ref), (shift_hbm, shift_ref), (center_hbm, center_ref),
            (spread_hbm, spread_ref), (gain_hbm, gain_ref), (x_hbm, x_ref),
        ))
    ]
    for copy in inputs:
        copy.start()
    v_rows, width = x_ref.shape
    x_block = w_ref.shape[0]
    x_half = x_block // halves
    grain = x_half // 4
    sub_rows = v_rows // subs
    total = nz * subs
    piece = cap * sub_rows
    slots = nz * piece
    x_part = g_out.shape[0]
    l_sub, l_subs, l_piece = log2(sub_rows), log2(subs), log2(piece)

    barrier = pltpu.get_barrier_semaphore()
    for d in range(1, nz):
        pl.semaphore_signal(
            barrier, inc=1, device_id={"slab": lax.rem(z + d, nz)}, device_id_type=MESH
        )
    for d in range(1, na):
        pl.semaphore_signal(
            barrier, inc=1, device_id={"ang": lax.rem(a + d, na)}, device_id_type=MESH
        )
    pl.semaphore_signal(barrier, inc=1, device_id={"parts": 1 - p}, device_id_type=MESH)
    pl.semaphore_signal(barrier, inc=1, device_id={"chan": 1 - c}, device_id_type=MESH)

    pl.semaphore_wait(barrier, nz - 1 + na - 1 + 2)

    def weight_copy(s, h, qp, qc, ss, rs, device, src=None):
        start = s * x_block + h * x_half + (qp * 2 + qc) * grain
        block = w_full.at[pl.ds(pl.multiple_of(start, grain), grain)]
        return pltpu.make_async_remote_copy(
            src_ref=block if src is None else src, dst_ref=block,
            send_sem=ss.at[s * halves + h], recv_sem=rs.at[s * halves + h],
            device_id=device, device_id_type=MESH,
        )

    def up(s, h, src=None):
        return weight_copy(s, h, p, c, up_ss, wz_rs, {"slab": lax.rem(z + 1, nz)}, src)

    def down(s, h, src=None):
        return weight_copy(s, h, p, c, down_ss, wz_rs, {"slab": lax.rem(z + nz - 1, nz)}, src)

    def across(s, h, qp=p):
        return weight_copy(s, h, qp, c, wy_ss, wy_rs, {"parts": 1 - p})

    def twin(s, h, qc=c):
        return weight_copy(s, h, p, qc, wc_ss, wc_rs, {"chan": 1 - c})

    def twin_far(s, h, qc=c):
        return weight_copy(s, h, 1 - p, qc, wd_ss, wd_rs, {"chan": 1 - c})

    for h in range(halves):
        start = h * x_half + (p * 2 + c) * grain
        own = w_ref.at[pl.ds(pl.multiple_of(start, grain), grain)]

        @pl.when(z + 1 < nz)
        def _():
            up(z, h, own).start()

        @pl.when(z > 0)
        def _():
            down(z, h, own).start()

    own_copy = pltpu.make_async_copy(
        w_ref, w_full.at[pl.ds(pl.multiple_of(z * x_block, x_block), x_block)], own_sem
    )
    own_copy.start()

    for copy in inputs[:-1]:
        copy.wait()
    t_row = targets_ref[...].astype(F32)
    eye = iota((total, total), 0) == iota((total, total), 1)
    t_col = jnp.sum(keep(eye, jnp.broadcast_to(t_row, (total, total))), axis=1, keepdims=True)
    meta[a, 0:1, :] = center_ref[...]
    meta[a, 1:2, :] = spread_ref[...]
    meta[a, 2:3, :] = gain_ref[...]
    meta[a, 3:4, 0:total] = t_row
    meta[a, 4:5, 0:total] = shift_ref[...]

    b_of_v = z * subs + (iota((total, v_rows), 1) >> l_sub)
    b_col = iota((total, v_rows), 0)
    t_wide = jnp.broadcast_to(t_col, (total, v_rows))
    t_v = jnp.sum(keep(b_col == b_of_v, t_wide), axis=0, keepdims=True)
    before = (t_wide == t_v) & (b_col >= z * subs) & (b_col < b_of_v)
    rank_v = jnp.sum(before.astype(F32), axis=0, keepdims=True)
    slot = iota((slots, v_rows), 0)
    v_id = iota((slots, v_rows), 1)
    pick = (
        (t_v == (slot >> l_piece).astype(F32))
        & (rank_v == ((slot & (piece - 1)) >> l_sub).astype(F32))
        & ((v_id & (sub_rows - 1)) == (slot & (sub_rows - 1)))
    )
    inputs[-1].wait()
    send_rows[...] = jnp.dot(
        pick.astype(F32).astype(BF16), x_ref[...], preferred_element_type=F32
    ).astype(BF16)

    def make_tile(src_a):
        t_r = meta[src_a, 3:4, 0:total]
        s_r = meta[src_a, 4:5, 0:total]
        t_c = jnp.sum(keep(eye, jnp.broadcast_to(t_r, (total, total))), axis=1, keepdims=True)
        b0, b1 = iota((total, total), 0), iota((total, total), 1)
        earlier = (t_c == t_r) & ((b0 >> l_subs) == (b1 >> l_subs)) & (b0 < b1)
        rank = jnp.sum(earlier.astype(F32), axis=0, keepdims=True)
        sl = iota((slots, total), 0)
        b = iota((slots, total), 1)
        match = (
            ((b >> l_subs) == (sl >> l_piece))
            & (t_r == z.astype(F32))
            & (rank == ((sl & (piece - 1)) >> l_sub).astype(F32))
        )
        shift = jnp.sum(keep(match, jnp.broadcast_to(s_r, (slots, total))), axis=1, keepdims=True)
        j = (iota((slots, 1), 0) & (sub_rows - 1)).astype(F32)
        pos[...] = j + 0.5 - shift
        center = meta[src_a, 0:1, :]
        spread = meta[src_a, 1:2, :]
        scale = meta[src_a, 2:3, :] * lax.rsqrt(spread)
        inverse = 1.0 / spread
        step = min(32, slots)

        @pl.loop(0, slots // step)
        def _(i):
            at = pl.multiple_of(i * step, step)
            offset = (pos[pl.ds(at, step), :] - center) * inverse
            tile_out[pl.ds(pl.multiple_of(src_a * slots + at, step), step), :] = (
                scale / (1.0 + offset * offset)
            ).astype(BF16)

    def row_copy(src_z, dst_z):
        return pltpu.make_async_remote_copy(
            src_ref=send_rows.at[pl.ds(pl.multiple_of(dst_z * piece, piece), piece)],
            dst_ref=rows.at[pl.ds(pl.multiple_of(src_z * piece, piece), piece)],
            send_sem=row_ss.at[dst_z], recv_sem=row_rs.at[src_z],
            device_id={"slab": dst_z}, device_id_type=MESH,
        )

    row_copy(z, lax.rem(z + nz // 2, nz)).start()

    def meta_copy(src_a, dst_a):
        return pltpu.make_async_remote_copy(
            src_ref=meta.at[src_a], dst_ref=meta.at[src_a],
            send_sem=meta_ss.at[dst_a], recv_sem=meta_rs.at[src_a],
            device_id={"ang": dst_a}, device_id_type=MESH,
        )

    for d in range(1, na):
        meta_copy(a, lax.rem(a + d, na)).start()

    mine = pl.ds(pl.multiple_of(z * piece, piece), piece)
    rows[mine, :] = send_rows[mine, :]


    parts_of = nz // na

    def g_copy(s, h, src_a, dst_a):
        near = lax.rem(s, parts_of)
        at = pl.multiple_of(near * x_block + h * x_half, x_half)
        return pltpu.make_async_remote_copy(
            src_ref=w_proj.at[pl.ds(pl.multiple_of(s * x_block + h * x_half, x_half), x_half)],
            dst_ref=g_recv.at[src_a, pl.ds(at, x_half)],
            send_sem=g_ss.at[s * halves + h],
            recv_sem=g_rs.at[(src_a * parts_of + near) * halves + h],
            device_id={"ang": dst_a}, device_id_type=MESH,
        )

    def project(s, h):
        at = pl.ds(pl.multiple_of(s * x_block + h * x_half, x_half), x_half)
        block = lax.dot_general(
            w_full[at, :], rows[...], (((1,), (1,)), ((), ())), preferred_element_type=F32
        ).astype(BF16)
        dst_a = s // parts_of

        @pl.when(dst_a != a)
        def _():
            w_proj[at, :] = block
            g_copy(s, h, a, dst_a).start()

        @pl.when(dst_a == a)
        def _():
            here = lax.rem(s, parts_of) * x_block + h * x_half
            g_recv[a, pl.ds(pl.multiple_of(here, x_half), x_half), :] = block

    pace = [d for d in range(nz - 1, 0, -1) if d != nz // 2]
    def pass_on(t, h):
        below, above = z - t, z + t

        @pl.when(below >= 0)
        def _():
            up(below, h).wait_recv()

            @pl.when(z + 1 < nz)
            def _():
                up(below, h).start()

            across(below, h).start()
            twin(below, h).start()

        @pl.when(above < nz)
        def _():
            down(above, h).wait_recv()

            @pl.when(z > 0)
            def _():
                down(above, h).start()

            across(above, h).start()
            twin(above, h).start()

    def pass_to_twin(t, h):
        for s in (z - t, z + t):
            @pl.when((s >= 0) & (s < nz))
            def _():
                across(s, h, 1 - p).wait_recv()
                twin_far(s, h).start()

    def finish(t, h):
        for s in (z - t, z + t):
            @pl.when((s >= 0) & (s < nz))
            def _():
                twin(s, h, 1 - c).wait_recv()
                twin_far(s, h, 1 - c).wait_recv()
                project(s, h)

    steps = [(t, h) for t in range(1, nz) for h in range(halves)]
    ready = 2 * halves - 1
    done = 0
    for i, step in enumerate(steps):
        pass_on(*step)
        if i == halves - 1:
            for d in pace:
                row_copy(z, lax.rem(z + d, nz)).start()
        if i:
            pass_to_twin(*steps[i - 1])
        if i == halves - 1:
            make_tile(a)
        if i == halves:
            for d in range(1, na):
                src_a = lax.rem(a + d, na)
                meta_copy(src_a, a).wait_recv()
                make_tile(src_a)
        if i == ready:
            for d in range(1, nz):
                row_copy(lax.rem(z + d, nz), z).wait_recv()
            own_copy.wait()
            for h in range(halves):
                project(z, h)
        if i >= ready:
            while done < i - 1:
                finish(*steps[done])
                done += 1
    pass_to_twin(*steps[-1])
    for step in steps[done:]:
        finish(*step)

    for d in range(1, na):
        src_a = lax.rem(a + d, na)
        for k in range(parts_of):
            for h in range(halves):
                g_copy(a * parts_of + k, h, src_a, a).wait_recv()
    for k in range(na):
        g_out[:, k * slots:(k + 1) * slots] = g_recv[k]

    for d in range(1, nz):
        row_copy(z, lax.rem(z + d, nz)).wait_send()
    for d in range(1, na):
        meta_copy(a, lax.rem(a + d, na)).wait_send()
    for s in range(nz):
        @pl.when(s // parts_of != a)
        def _():
            for h in range(halves):
                g_copy(s, h, a, s // parts_of).wait_send()

        for h in range(halves):
            @pl.when((s <= z) & (z + 1 < nz))
            def _():
                up(s, h).wait_send()

            @pl.when((s >= z) & (z > 0))
            def _():
                down(s, h).wait_send()

            @pl.when(s != z)
            def _():
                across(s, h).wait_send()
                twin(s, h).wait_send()
                twin_far(s, h).wait_send()


def shards(sinogram, transaxial, targets, row_shift, center, spread, gain):
    nz = lax.axis_size("slab")
    na = lax.axis_size("ang")
    detector = sinogram[0, 0]
    weights = transaxial[0]
    v_rows, width = detector.shape
    total = targets.shape[1]
    subs = total // nz
    sub_rows = v_rows // subs
    cap = max(2, 2 * subs // nz)
    piece = cap * sub_rows
    slots = nz * piece
    x_all = weights.shape[0] * nz
    x_part = x_all // na
    r_rows = center.shape[1]
    halves = max(1, min(2, weights.shape[0] // 4 // 16))
    vmem = pl.BlockSpec(memory_space=pltpu.VMEM)
    dma = pltpu.SemaphoreType.DMA
    projected, tile = pl.pallas_call(
        functools.partial(kernel, nz, na, subs, cap, halves),
        out_shape=(
            jax.ShapeDtypeStruct((x_part, na * slots), BF16),
            jax.ShapeDtypeStruct((na * slots, r_rows), BF16),
        ),
        in_specs=[pl.BlockSpec(memory_space=pl.ANY)] * 7,
        out_specs=(vmem, vmem),
        scratch_shapes=[
            pltpu.VMEM((v_rows, width), BF16),
            pltpu.VMEM((1, total), jnp.int32),
            pltpu.VMEM((1, total), F32),
            pltpu.VMEM((1, r_rows), F32),
            pltpu.VMEM((1, r_rows), F32),
            pltpu.VMEM((1, r_rows), F32),
            pltpu.VMEM((x_all, width), BF16),
            pltpu.VMEM((slots, width), BF16),
            pltpu.VMEM((slots, width), BF16),
            pltpu.VMEM((x_all, slots), BF16),
            pltpu.VMEM((na, x_part, slots), BF16),
            pltpu.VMEM((na, 8, r_rows), F32),
            pltpu.VMEM((slots, 1), F32),
            dma((6,)),
            dma(()),
        ] + [dma((nz,))] * 2 + [dma((nz * halves,))] * 9 + [dma((na,))] * 2 + [dma((nz * halves,))] * 2,
        compiler_params=pltpu.CompilerParams(
            collective_id=0, has_side_effects=True, vmem_limit_bytes=60 * 1024 * 1024
        ),
    )(detector, weights, targets[..., 0], row_shift, center, spread, gain)
    volume = jnp.dot(projected, tile, preferred_element_type=F32)
    return volume[None]


def solution(mesh):
    assert mesh.shape["parts"] == 2 and mesh.shape["chan"] == 2
    in_specs = (
        P(("parts", "chan"), "ang", "slab", None),
        P("ang", "slab", None),
        P("ang", None, None),
        P("ang", None),
        P("ang", "slab"),
        P("ang", "slab"),
        P("ang", "slab"),
    )
    out_specs = P(("parts", "chan"), "ang", "slab")
    return jax.shard_map(shards, mesh=mesh, in_specs=in_specs, out_specs=out_specs, check_vma=False)
```

```python
import functools

import jax
import jax.numpy as jnp
from jax import lax
from jax.experimental import pallas as pl
from jax.experimental.pallas import tpu as pltpu
from jax.sharding import PartitionSpec as P

MESH = pl.DeviceIdType.MESH
F32 = jnp.float32
BF16 = jnp.bfloat16


def log2(n):
    assert n & (n - 1) == 0
    return n.bit_length() - 1


def iota(shape, dim):
    return lax.broadcasted_iota(jnp.int32, shape, dim)


def keep(mask, value):
    return jnp.where(mask, value, jnp.zeros_like(value))


def kernel(
    nz, na, subs, cap, halves,
    x_hbm, w_ref, targets_hbm, shift_hbm, center_hbm, spread_hbm, gain_hbm,
    g_out, tile_out,
    x_ref, targets_ref, shift_ref, center_ref, spread_ref, gain_ref,
    w_full, send_rows, rows, w_proj, g_recv, meta, pos,
    in_sem, own_sem, row_ss, row_rs, up_ss, down_ss, wz_rs, wy_ss, wy_rs, wc_ss, wc_rs,
    wd_ss, wd_rs, meta_ss, meta_rs, g_ss, g_rs,
):
    p = lax.axis_index("parts")
    z = lax.axis_index("slab")
    a = lax.axis_index("ang")
    c = lax.axis_index("chan")
    inputs = [
        pltpu.make_async_copy(src, dst, in_sem.at[i])
        for i, (src, dst) in enumerate((
            (targets_hbm, targets_ref), (shift_hbm, shift_ref), (center_hbm, center_ref),
            (spread_hbm, spread_ref), (gain_hbm, gain_ref), (x_hbm, x_ref),
        ))
    ]
    for copy in inputs:
        copy.start()
    v_rows, width = x_ref.shape
    x_block = w_ref.shape[0]
    x_half = x_block // halves
    grain = x_half // 4
    sub_rows = v_rows // subs
    total = nz * subs
    piece = cap * sub_rows
    slots = nz * piece
    x_part = g_out.shape[0]
    l_sub, l_subs, l_piece = log2(sub_rows), log2(subs), log2(piece)

    barrier = pltpu.get_barrier_semaphore()
    for d in range(1, nz):
        pl.semaphore_signal(
            barrier, inc=1, device_id={"slab": lax.rem(z + d, nz)}, device_id_type=MESH
        )
    for d in range(1, na):
        pl.semaphore_signal(
            barrier, inc=1, device_id={"ang": lax.rem(a + d, na)}, device_id_type=MESH
        )
    pl.semaphore_signal(barrier, inc=1, device_id={"parts": 1 - p}, device_id_type=MESH)
    pl.semaphore_signal(barrier, inc=1, device_id={"chan": 1 - c}, device_id_type=MESH)

    pl.semaphore_wait(barrier, nz - 1 + na - 1 + 2)

    def weight_copy(s, h, qp, qc, ss, rs, device, src=None):
        start = s * x_block + h * x_half + (qp * 2 + qc) * grain
        block = w_full.at[pl.ds(pl.multiple_of(start, grain), grain)]
        return pltpu.make_async_remote_copy(
            src_ref=block if src is None else src, dst_ref=block,
            send_sem=ss.at[s * halves + h], recv_sem=rs.at[s * halves + h],
            device_id=device, device_id_type=MESH,
        )

    def up(s, h, src=None):
        return weight_copy(s, h, p, c, up_ss, wz_rs, {"slab": lax.rem(z + 1, nz)}, src)

    def down(s, h, src=None):
        return weight_copy(s, h, p, c, down_ss, wz_rs, {"slab": lax.rem(z + nz - 1, nz)}, src)

    def across(s, h, qp=p):
        return weight_copy(s, h, qp, c, wy_ss, wy_rs, {"parts": 1 - p})

    def twin(s, h, qc=c):
        return weight_copy(s, h, p, qc, wc_ss, wc_rs, {"chan": 1 - c})

    def twin_far(s, h, qc=c):
        return weight_copy(s, h, 1 - p, qc, wd_ss, wd_rs, {"chan": 1 - c})

    for h in range(halves):
        start = h * x_half + (p * 2 + c) * grain
        own = w_ref.at[pl.ds(pl.multiple_of(start, grain), grain)]

        @pl.when(z + 1 < nz)
        def _():
            up(z, h, own).start()

        @pl.when(z > 0)
        def _():
            down(z, h, own).start()

    own_copy = pltpu.make_async_copy(
        w_ref, w_full.at[pl.ds(pl.multiple_of(z * x_block, x_block), x_block)], own_sem
    )
    own_copy.start()

    for copy in inputs[:-1]:
        copy.wait()
    t_row = targets_ref[...].astype(F32)
    eye = iota((total, total), 0) == iota((total, total), 1)
    t_col = jnp.sum(keep(eye, jnp.broadcast_to(t_row, (total, total))), axis=1, keepdims=True)
    meta[a, 0:1, :] = center_ref[...]
    meta[a, 1:2, :] = spread_ref[...]
    meta[a, 2:3, :] = gain_ref[...]
    meta[a, 3:4, 0:total] = t_row
    meta[a, 4:5, 0:total] = shift_ref[...]

    b_of_v = z * subs + (iota((total, v_rows), 1) >> l_sub)
    b_col = iota((total, v_rows), 0)
    t_wide = jnp.broadcast_to(t_col, (total, v_rows))
    t_v = jnp.sum(keep(b_col == b_of_v, t_wide), axis=0, keepdims=True)
    before = (t_wide == t_v) & (b_col >= z * subs) & (b_col < b_of_v)
    rank_v = jnp.sum(before.astype(F32), axis=0, keepdims=True)
    slot = iota((slots, v_rows), 0)
    v_id = iota((slots, v_rows), 1)
    pick = (
        (t_v == (slot >> l_piece).astype(F32))
        & (rank_v == ((slot & (piece - 1)) >> l_sub).astype(F32))
        & ((v_id & (sub_rows - 1)) == (slot & (sub_rows - 1)))
    )
    inputs[-1].wait()
    send_rows[...] = jnp.dot(
        pick.astype(F32).astype(BF16), x_ref[...], preferred_element_type=F32
    ).astype(BF16)

    def make_tile(src_a):
        t_r = meta[src_a, 3:4, 0:total]
        s_r = meta[src_a, 4:5, 0:total]
        t_c = jnp.sum(keep(eye, jnp.broadcast_to(t_r, (total, total))), axis=1, keepdims=True)
        b0, b1 = iota((total, total), 0), iota((total, total), 1)
        earlier = (t_c == t_r) & ((b0 >> l_subs) == (b1 >> l_subs)) & (b0 < b1)
        rank = jnp.sum(earlier.astype(F32), axis=0, keepdims=True)
        sl = iota((slots, total), 0)
        b = iota((slots, total), 1)
        match = (
            ((b >> l_subs) == (sl >> l_piece))
            & (t_r == z.astype(F32))
            & (rank == ((sl & (piece - 1)) >> l_sub).astype(F32))
        )
        shift = jnp.sum(keep(match, jnp.broadcast_to(s_r, (slots, total))), axis=1, keepdims=True)
        j = (iota((slots, 1), 0) & (sub_rows - 1)).astype(F32)
        pos[...] = j + 0.5 - shift
        center = meta[src_a, 0:1, :]
        spread = meta[src_a, 1:2, :]
        scale = meta[src_a, 2:3, :] * lax.rsqrt(spread)
        inverse = 1.0 / spread
        step = min(32, slots)

        @pl.loop(0, slots // step)
        def _(i):
            at = pl.multiple_of(i * step, step)
            offset = (pos[pl.ds(at, step), :] - center) * inverse
            tile_out[pl.ds(pl.multiple_of(src_a * slots + at, step), step), :] = (
                scale / (1.0 + offset * offset)
            ).astype(BF16)

    def row_copy(src_z, dst_z):
        return pltpu.make_async_remote_copy(
            src_ref=send_rows.at[pl.ds(pl.multiple_of(dst_z * piece, piece), piece)],
            dst_ref=rows.at[pl.ds(pl.multiple_of(src_z * piece, piece), piece)],
            send_sem=row_ss.at[dst_z], recv_sem=row_rs.at[src_z],
            device_id={"slab": dst_z}, device_id_type=MESH,
        )

    row_copy(z, lax.rem(z + nz // 2, nz)).start()

    def meta_copy(src_a, dst_a):
        return pltpu.make_async_remote_copy(
            src_ref=meta.at[src_a], dst_ref=meta.at[src_a],
            send_sem=meta_ss.at[dst_a], recv_sem=meta_rs.at[src_a],
            device_id={"ang": dst_a}, device_id_type=MESH,
        )

    for d in range(1, na):
        meta_copy(a, lax.rem(a + d, na)).start()

    mine = pl.ds(pl.multiple_of(z * piece, piece), piece)
    rows[mine, :] = send_rows[mine, :]


    parts_of = nz // na

    def g_copy(s, h, src_a, dst_a):
        near = lax.rem(s, parts_of)
        at = pl.multiple_of(near * x_block + h * x_half, x_half)
        return pltpu.make_async_remote_copy(
            src_ref=w_proj.at[pl.ds(pl.multiple_of(s * x_block + h * x_half, x_half), x_half)],
            dst_ref=g_recv.at[src_a, pl.ds(at, x_half)],
            send_sem=g_ss.at[s * halves + h],
            recv_sem=g_rs.at[(src_a * parts_of + near) * halves + h],
            device_id={"ang": dst_a}, device_id_type=MESH,
        )

    def project(s, h):
        at = pl.ds(pl.multiple_of(s * x_block + h * x_half, x_half), x_half)
        block = lax.dot_general(
            w_full[at, :], rows[...], (((1,), (1,)), ((), ())), preferred_element_type=F32
        ).astype(BF16)
        dst_a = s // parts_of

        @pl.when(dst_a != a)
        def _():
            w_proj[at, :] = block
            g_copy(s, h, a, dst_a).start()

        @pl.when(dst_a == a)
        def _():
            here = lax.rem(s, parts_of) * x_block + h * x_half
            g_recv[a, pl.ds(pl.multiple_of(here, x_half), x_half), :] = block

    pace = [d for d in range(nz - 1, 0, -1) if d != nz // 2]
    def pass_on(t, h):
        below, above = z - t, z + t

        @pl.when(below >= 0)
        def _():
            up(below, h).wait_recv()

            @pl.when(z + 1 < nz)
            def _():
                up(below, h).start()

            across(below, h).start()
            twin(below, h).start()

        @pl.when(above < nz)
        def _():
            down(above, h).wait_recv()

            @pl.when(z > 0)
            def _():
                down(above, h).start()

            across(above, h).start()
            twin(above, h).start()

    def pass_to_twin(t, h):
        for s in (z - t, z + t):
            @pl.when((s >= 0) & (s < nz))
            def _():
                across(s, h, 1 - p).wait_recv()
                twin_far(s, h).start()

    def finish(t, h):
        for s in (z - t, z + t):
            @pl.when((s >= 0) & (s < nz))
            def _():
                twin(s, h, 1 - c).wait_recv()
                twin_far(s, h, 1 - c).wait_recv()
                project(s, h)

    steps = [(t, h) for t in range(1, nz) for h in range(halves)]
    ready = 2 * halves - 1
    done = 0
    for i, step in enumerate(steps):
        pass_on(*step)
        if i == halves - 1:
            for d in pace:
                row_copy(z, lax.rem(z + d, nz)).start()
        if i:
            pass_to_twin(*steps[i - 1])
        if i == halves - 1:
            make_tile(a)
        if i == halves:
            for d in range(1, na):
                src_a = lax.rem(a + d, na)
                meta_copy(src_a, a).wait_recv()
                make_tile(src_a)
        if i == ready:
            for d in range(1, nz):
                row_copy(lax.rem(z + d, nz), z).wait_recv()
            own_copy.wait()
            for h in range(halves):
                project(z, h)
        if i >= ready:
            while done < i - 1:
                finish(*steps[done])
                done += 1
    pass_to_twin(*steps[-1])
    for step in steps[done:]:
        finish(*step)

    g_out[:, pl.ds(pl.multiple_of(a * slots, slots), slots)] = g_recv[a]
    for d in range(1, na):
        src_a = lax.rem(a + d, na)
        for k in range(parts_of):
            for h in range(halves):
                g_copy(a * parts_of + k, h, src_a, a).wait_recv()
        g_out[:, pl.ds(pl.multiple_of(src_a * slots, slots), slots)] = g_recv[src_a]

    for d in range(1, nz):
        row_copy(z, lax.rem(z + d, nz)).wait_send()
    for d in range(1, na):
        meta_copy(a, lax.rem(a + d, na)).wait_send()
    for s in range(nz):
        @pl.when(s // parts_of != a)
        def _():
            for h in range(halves):
                g_copy(s, h, a, s // parts_of).wait_send()

        for h in range(halves):
            @pl.when((s <= z) & (z + 1 < nz))
            def _():
                up(s, h).wait_send()

            @pl.when((s >= z) & (z > 0))
            def _():
                down(s, h).wait_send()

            @pl.when(s != z)
            def _():
                across(s, h).wait_send()
                twin(s, h).wait_send()
                twin_far(s, h).wait_send()


def shards(sinogram, transaxial, targets, row_shift, center, spread, gain):
    nz = lax.axis_size("slab")
    na = lax.axis_size("ang")
    detector = sinogram[0, 0]
    weights = transaxial[0]
    v_rows, width = detector.shape
    total = targets.shape[1]
    subs = total // nz
    sub_rows = v_rows // subs
    cap = max(2, 2 * subs // nz)
    piece = cap * sub_rows
    slots = nz * piece
    x_all = weights.shape[0] * nz
    x_part = x_all // na
    r_rows = center.shape[1]
    halves = max(1, min(2, weights.shape[0] // 4 // 16))
    vmem = pl.BlockSpec(memory_space=pltpu.VMEM)
    dma = pltpu.SemaphoreType.DMA
    projected, tile = pl.pallas_call(
        functools.partial(kernel, nz, na, subs, cap, halves),
        out_shape=(
            jax.ShapeDtypeStruct((x_part, na * slots), BF16),
            jax.ShapeDtypeStruct((na * slots, r_rows), BF16),
        ),
        in_specs=[pl.BlockSpec(memory_space=pl.ANY)] * 7,
        out_specs=(vmem, vmem),
        scratch_shapes=[
            pltpu.VMEM((v_rows, width), BF16),
            pltpu.VMEM((1, total), jnp.int32),
            pltpu.VMEM((1, total), F32),
            pltpu.VMEM((1, r_rows), F32),
            pltpu.VMEM((1, r_rows), F32),
            pltpu.VMEM((1, r_rows), F32),
            pltpu.VMEM((x_all, width), BF16),
            pltpu.VMEM((slots, width), BF16),
            pltpu.VMEM((slots, width), BF16),
            pltpu.VMEM((x_all, slots), BF16),
            pltpu.VMEM((na, x_part, slots), BF16),
            pltpu.VMEM((na, 8, r_rows), F32),
            pltpu.VMEM((slots, 1), F32),
            dma((6,)),
            dma(()),
        ] + [dma((nz,))] * 2 + [dma((nz * halves,))] * 9 + [dma((na,))] * 2 + [dma((nz * halves,))] * 2,
        compiler_params=pltpu.CompilerParams(
            collective_id=0, has_side_effects=True, vmem_limit_bytes=60 * 1024 * 1024
        ),
    )(detector, weights, targets[..., 0], row_shift, center, spread, gain)
    volume = jnp.dot(projected, tile, preferred_element_type=F32)
    return volume[None]


def solution(mesh):
    assert mesh.shape["parts"] == 2 and mesh.shape["chan"] == 2
    in_specs = (
        P(("parts", "chan"), "ang", "slab", None),
        P("ang", "slab", None),
        P("ang", None, None),
        P("ang", None),
        P("ang", "slab"),
        P("ang", "slab"),
        P("ang", "slab"),
    )
    out_specs = P(("parts", "chan"), "ang", "slab")
    return jax.shard_map(shards, mesh=mesh, in_specs=in_specs, out_specs=out_specs, check_vma=False)
```
